128 devices in a mesh: elem: 128 (over x, y, z, core).
Axes of the slice: x: 4, y: 4, z: 4, core: 2. Of those that a mesh axis runs over, the one named last changes fastest.
Arguments:
- solution: bfloat16 [5, 216, 524288], P(None, None, 'elem'), may hold values from -6 to 6
- wind_field: bfloat16 [3, 216, 524288], P(None, None, 'elem'), may hold values from -6 to 6
- metric_scale: float32 [524288], P('elem'), may hold values from 0.5 to 4
- neighbours: int32 [6, 524288], P(None, 'elem'), may hold values from 0 to 5119
- precursor: bfloat16 [5, 216, 32768], P(None, None, 'elem'), may hold values from -6 to 6
- mortar_send: int32 [128, 2, 1024], P('elem'), may hold values from -1 to 255, as said below
- fringe_table: int32 [3, 65536], P(None, 'elem'), may hold values from 0 to 4095, as said below
- volume_operator_stack: bfloat16 [3, 216, 216], replicated, may hold values from -0.4375 to 0.4375
- surface_lift_weight: bfloat16 [216, 216], replicated, may hold values from -0.4375 to 0.4375
- mortar_proj: bfloat16 [4, 36, 216], replicated, may hold values from -0.4375 to 0.4375
Outputs:
- section_rate: bfloat16 [5, 216, 524288], P(None, None, 'elem')
The draws below stay inside these ranges and needn't reach their ends.
Inputs may be any that keep to these rules, and one draw needn't show every extreme that they name: `mortar_send`: on partition s, entry [0, d * 8 + c] names the local precursor element that s sends to partition d in its slot c, or -1 where that slot is empty; entry [1, d * 8 + c] is that mortar's type, 0 in empty slots. Every partition receives all 8 slots from at least one partition. `fringe_table`: on partition d, column j: row 0 is the position s * 8 + c of a live slot c that partition s sends to d, distinct within d; row 1 a local element, distinct within d, whose face 0 meets the precursor block; row 2 the mortar type, equal to entry [1, d * 8 + c] of mortar_send on s. `neighbours`: entry [f, e] is the position of the element across face f of local element e in the partition's extended block: below 512 the previous partition's last 512 elements, 512 + i local element i, from 4608 on the next partition's first 512 elements. That element meets face f with its opposite face, nodes aligned.
All inputs are finite; a program needn't handle non-finite values.
Results may differ from the reference program's by a relative error of at most 0.005.
Values may be sent and summed in bfloat16 or wider, within the bound.
No kernel may reach another device: no remote copies, remote signals or barrier semaphores. Data moves between devices by JAX's collectives and lax.ppermute only.
A program may use at most 256 MiB of HBM per device.

```python
import math
import jax
import jax.numpy as jnp
from jax import lax

NV = 5
EDGE_NODES = 6
NODES = 216
FACE_NODES = 36
MTYPES = 4
E_DEV = 4096
BAND = 512
FRINGE_PER_PART = 512
PREC_DEV = 256
CAP = 8
ELEMS = 524288
PRECURSORS = 32768
N_ELEM = 128


def mortar_plan(key):
    base = jax.random.fold_in(key, 4021)
    key_score, forcing_key, key_local, key_kind, key_elem = jax.random.split(base, 5)
    slot_count = N_ELEM * CAP
    position = jnp.arange(slot_count, dtype=jnp.int32)
    turbine_source = position // CAP
    random_score = jax.random.randint(key_score, (N_ELEM, slot_count), 0, 4096, dtype=jnp.int32)
    source_bias = turbine_source * 8192 // N_ELEM
    scores = (random_score + source_bias[None, :]) * slot_count + position[None, :]
    forced = jax.random.randint(forcing_key, (N_ELEM,), 0, N_ELEM, dtype=jnp.int32)
    scores = jnp.where(turbine_source[None, :] == forced[:, None], position[None, :] - slot_count, scores)
    ranking = jnp.argsort(scores, axis=1, stable=True)
    picked = ranking[:, :FRINGE_PER_PART].astype(jnp.int32)
    local_ids = jax.random.randint(key_local, (N_ELEM, FRINGE_PER_PART), 0, PREC_DEV, dtype=jnp.int32)
    mortar_kinds = jax.random.randint(key_kind, (N_ELEM, FRINGE_PER_PART), 0, MTYPES, dtype=jnp.int32)
    elem_scores = jax.random.randint(key_elem, (N_ELEM, E_DEV), 0, 131072, dtype=jnp.int32) * E_DEV + jnp.arange(E_DEV, dtype=jnp.int32)[None, :]
    elements = jnp.argsort(elem_scores, axis=1, stable=True)[:, :FRINGE_PER_PART].astype(jnp.int32)
    return (picked, local_ids, mortar_kinds, elements)


def draw_mortar_send(key, part):
    picked, local_ids, mortar_kinds, elements = mortar_plan(key)
    slot_count = N_ELEM * CAP
    receiver = jnp.broadcast_to(jnp.arange(N_ELEM, dtype=jnp.int32)[:, None], picked.shape)
    turbine_source = picked // CAP
    column_list = receiver * CAP + picked % CAP
    send_index = jnp.full((N_ELEM, slot_count), -1, jnp.int32).at[turbine_source, column_list].set(local_ids)
    send_kind = jnp.zeros((N_ELEM, slot_count), jnp.int32).at[turbine_source, column_list].set(mortar_kinds)
    return jnp.stack([send_index, send_kind], axis=1)


def draw_fringe_table(key, part):
    picked, local_ids, mortar_kinds, elements = mortar_plan(key)
    return jnp.stack([picked, elements, mortar_kinds], axis=0).reshape(3, N_ELEM * FRINGE_PER_PART)


def place_ends(drawn, stream_key, least, largest):
    longest = drawn.shape.index(max(drawn.shape))
    spots = []
    for shift in (0, 1):
        where = [jax.random.randint(jax.random.fold_in(stream_key, axis), (), 0, length) for axis, length in enumerate(drawn.shape)]
        where[longest] = (where[longest] + shift) % drawn.shape[longest]
        spots.append(tuple(where))
    return drawn.at[spots[0]].set(least).at[spots[1]].set(largest)


def shard_levels(rng, dims, cuts, least, top_value):
    def one(dim, shards_of):
        heights = jax.random.uniform(jax.random.fold_in(jax.random.fold_in(rng, 6), dim), (shards_of,), jnp.float32, least / len(cuts), top_value / len(cuts))
        return jnp.repeat(jnp.exp(heights), dims[dim] // shards_of).reshape((-1,) + (1,) * (len(dims) - dim - 1))

    level = one(*cuts[0])
    for cut in cuts[1:]:
        level = level * one(*cut)
    return level


def normal_values(stream_key, shape, deviation, limit, cuts=(), kind=jnp.bfloat16):
    entries = deviation * jax.random.normal(stream_key, shape, jnp.float32)
    if cuts:
        entries = entries * shard_levels(stream_key, shape, cuts, -0.22, 0.18)
    return jnp.clip(entries, -limit, limit).astype(kind)


def setup_inputs(seed: int = 0) -> dict:
    splits = jax.random.split(jax.random.key(seed), 11)
    solution = normal_values(splits[0], (NV, NODES, ELEMS), 1.0, 6.0, ((2, 128),))
    wind_field = normal_values(splits[1], (3, NODES, ELEMS), 1.0, 6.0, ((2, 128),))
    metric_scale = jnp.clip(jnp.exp(math.log(4.0) - 2.0794415 * jax.random.uniform(splits[2], (ELEMS,), jnp.float32) ** shard_levels(splits[2], (ELEMS,), ((0, 128),), -0.2, 0.2)), 0.5, 4.0)
    neighbours = place_ends(jax.random.randint(splits[3], (6, ELEMS), 0, E_DEV + 2 * BAND), jax.random.fold_in(splits[3], 1), 0, (E_DEV + 2 * BAND) - 1).astype(jnp.int32)
    precursor = normal_values(splits[4], (NV, NODES, PRECURSORS), 1.0, 6.0, ((2, 128),))
    mortar_send = draw_mortar_send(jax.random.fold_in(splits[10], 71), 0)
    fringe_table = draw_fringe_table(jax.random.fold_in(splits[10], 71), 0)
    volume_operator_stack = normal_values(splits[7], (3, NODES, NODES), NODES ** -0.5, 0.4375)
    surface_lift_weight = normal_values(splits[8], (NODES, NODES), NODES ** -0.5, 0.4375)
    mortar_proj = normal_values(splits[9], (MTYPES, FACE_NODES, NODES), NODES ** -0.5, 0.4375)
    return dict(solution=solution, wind_field=wind_field, metric_scale=metric_scale, neighbours=neighbours, precursor=precursor, mortar_send=mortar_send, fringe_table=fringe_table, volume_operator_stack=volume_operator_stack, surface_lift_weight=surface_lift_weight, mortar_proj=mortar_proj)


sound_speed = 1.0


def face_traces(nodal_state_values):
    channels = nodal_state_values.shape[0]
    elem_count = nodal_state_values.shape[-1]
    lattice = nodal_state_values.reshape(channels, EDGE_NODES, EDGE_NODES, EDGE_NODES, elem_count)
    far_end = EDGE_NODES - 1
    face_list = [lattice[:, 0], lattice[:, far_end], lattice[:, :, 0], lattice[:, :, far_end],
                 lattice[:, :, :, 0], lattice[:, :, :, far_end]]
    return jnp.stack([item.reshape(channels, FACE_NODES, elem_count) for item in face_list], axis=1)


def project(blocks, mortar_kinds, mortar_proj):
    projected = jnp.einsum('tqn,vns->vtqs', mortar_proj.astype(jnp.float32), blocks.astype(jnp.float32))
    selector = (mortar_kinds[None, :] == jnp.arange(MTYPES, dtype=jnp.int32)[:, None]).astype(jnp.float32)
    return jnp.sum(projected * selector[None, :, None, :], axis=1).astype(jnp.bfloat16)


def element_rate(solution, extended, wind_field, metric_scale, neighbours, mortar_trace, fringe_elements, volume_operator_stack, surface_lift_weight):
    variables = solution.shape[0]
    elem_count = solution.shape[2]
    interior_trace = face_traces(solution)
    outer = face_traces(extended)
    beyond = jnp.stack([jnp.take(outer[:, face_id ^ 1], neighbours[face_id], axis=2) for face_id in range(6)], axis=1)
    first_face = beyond[:, 0].at[:, :, fringe_elements].set(mortar_trace)
    coupled = beyond.at[:, 0].set(first_face)
    wind_faces = face_traces(wind_field).astype(jnp.float32)
    speeds = jnp.stack([(2.0 * (face_id % 2) - 1.0) * wind_faces[face_id // 2, face_id] for face_id in range(6)], axis=0)
    coefficient = 0.5 * (speeds - jnp.abs(speeds) - sound_speed)
    surface_term = ((interior_trace.astype(jnp.float32) - coupled.astype(jnp.float32)) * coefficient[None])
    surface_term = surface_term.reshape(variables, 6 * FACE_NODES, elem_count).astype(jnp.bfloat16)
    numerical_flux = (wind_field.astype(jnp.float32)[:, None] * solution.astype(jnp.float32)[None]).astype(jnp.bfloat16)
    volume_term = jnp.einsum('phj,pijc->ihc', volume_operator_stack.astype(jnp.float32), numerical_flux.astype(jnp.float32))
    lifted_residual = jnp.einsum('hj,tjy->thy', surface_lift_weight.astype(jnp.float32), surface_term.astype(jnp.float32))
    return (metric_scale.astype(jnp.float32)[None, None, :] * (lifted_residual - volume_term)).astype(jnp.bfloat16)


def reference(solution, wind_field, metric_scale, neighbours, precursor, mortar_send, fringe_table, volume_operator_stack, surface_lift_weight, mortar_proj):
    receiver = jnp.arange(N_ELEM * FRINGE_PER_PART, dtype=jnp.int32) // FRINGE_PER_PART
    place = fringe_table[0]
    turbine_source = place // CAP
    slot_id = place % CAP
    local_id = mortar_send[turbine_source, 0, receiver * CAP + slot_id]
    column_list = (turbine_source * PREC_DEV + local_id).astype(jnp.int32)
    blocks = jnp.take(precursor, column_list, axis=2)
    mortar_all = project(blocks, fringe_table[2], mortar_proj)

    def partition(part_index):
        leading_element = part_index * E_DEV
        own_block = lax.dynamic_slice_in_dim(solution, leading_element, E_DEV, 2)
        prior_residual = lax.dynamic_slice_in_dim(solution, jnp.maximum(leading_element - BAND, 0).astype(jnp.int32), BAND, 2)
        prior_residual = jnp.where(part_index > 0, prior_residual, jnp.zeros_like(prior_residual))
        following = lax.dynamic_slice_in_dim(solution, jnp.minimum(leading_element + E_DEV, ELEMS - BAND).astype(jnp.int32), BAND, 2)
        following = jnp.where(part_index < N_ELEM - 1, following, jnp.zeros_like(following))
        extended = jnp.concatenate([prior_residual, own_block, following], axis=2)
        wind_part = lax.dynamic_slice_in_dim(wind_field, leading_element, E_DEV, 2)
        metric_part = lax.dynamic_slice_in_dim(metric_scale, leading_element, E_DEV, 0)
        neighbour_part = lax.dynamic_slice_in_dim(neighbours, leading_element, E_DEV, 1)
        fringe_first = part_index * FRINGE_PER_PART
        mortar_part = lax.dynamic_slice_in_dim(mortar_all, fringe_first, FRINGE_PER_PART, 2)
        fringe_part = lax.dynamic_slice_in_dim(fringe_table[1], fringe_first, FRINGE_PER_PART, 0)
        return element_rate(own_block, extended, wind_part, metric_part, neighbour_part, mortar_part, fringe_part, volume_operator_stack, surface_lift_weight)

    rates = lax.map(partition, jnp.arange(N_ELEM, dtype=jnp.int32))
    return jnp.transpose(rates, (1, 2, 0, 3)).reshape(NV, NODES, ELEMS)
```

```python
import functools

import jax
import jax.numpy as jnp
import numpy as np
from jax import lax
from jax.experimental import pallas as pl
from jax.experimental.pallas import tpu as pltpu
from jax.sharding import PartitionSpec as P

EDGE = 6
FACES = 6
FACE_NODES = 36
SLOT = 48
LANES = 128
ROW = 2 * LANES
BAND = 512
BLOCK = 256
UNROLL = 32
CAP_KINDS = 4
SOUND_SPEED = 1.0


def face_node_lists():
    grid = np.arange(EDGE**3).reshape(EDGE, EDGE, EDGE)
    end = EDGE - 1
    return [
        grid[0].ravel(),
        grid[end].ravel(),
        grid[:, 0].ravel(),
        grid[:, end].ravel(),
        grid[:, :, 0].ravel(),
        grid[:, :, end].ravel(),
    ]


def face_picker():
    pick = np.zeros((FACES * SLOT, EDGE**3), np.float32)
    for face, nodes in enumerate(face_node_lists()):
        pick[face * SLOT + np.arange(FACE_NODES), nodes] = 1.0
    return jnp.asarray(pick, dtype=jnp.bfloat16)


NT = (((1,), (1,)), ((), ()))


def mortar_kernel(combo_ref, precursor_ref, proj_ref, out_ref):
    variables, _, count = precursor_ref.shape
    slots = combo_ref.shape[0]
    combo = combo_ref[...]
    projected = [
        jnp.dot(proj_ref[...], precursor_ref[v], preferred_element_type=jnp.float32).astype(
            jnp.bfloat16
        )
        for v in range(variables)
    ]
    total = jnp.zeros((slots, ROW), jnp.float32)
    ids = lax.broadcasted_iota(jnp.int32, (slots, count), 1)
    pad = jnp.zeros((ROW - variables * SLOT, count), jnp.bfloat16)
    for kind in range(CAP_KINDS):
        table = jnp.concatenate(
            [item[kind * SLOT : (kind + 1) * SLOT] for item in projected] + [pad], axis=0
        )
        onehot = (combo == ids + kind * count).astype(jnp.float32).astype(jnp.bfloat16)
        total = total + lax.dot_general(onehot, table, NT, preferred_element_type=jnp.float32)
    out_ref[...] = total.astype(jnp.bfloat16)


def mortar_rows(precursor, mortar_send, mortar_proj):
    count = precursor.shape[2]
    combo = jnp.maximum(mortar_send[0, 0], 0) + mortar_send[0, 1] * count
    slots = combo.shape[0]
    proj = jnp.pad(mortar_proj, ((0, 0), (0, SLOT - FACE_NODES), (0, 0)))
    proj = proj.reshape(CAP_KINDS * SLOT, -1)
    return pl.pallas_call(
        mortar_kernel,
        out_shape=jax.ShapeDtypeStruct((slots, ROW), jnp.bfloat16),
        compiler_params=pltpu.CompilerParams(vmem_limit_bytes=32 << 20),
    )(combo[:, None], precursor, proj)


def rate_kernel(
    halo_blocks,
    own_blocks,
    index_hbm,
    fringe_ref,
    low_ref,
    high_ref,
    sol_ref,
    wind_ref,
    metric_ref,
    mortar_ref,
    pick_ref,
    weight_ref,
    eye_ref,
    out_ref,
    rows,
    got,
    operand,
    index,
    sem,
):
    step = pl.program_id(0)
    variables, nodes, _ = sol_ref.shape
    extended_blocks = own_blocks + 2 * halo_blocks
    face_rows = 2 * BLOCK * extended_blocks
    own = own_blocks * BLOCK
    traces = FACES * SLOT

    @pl.when(step == 0)
    def _():
        copy = pltpu.make_async_copy(index_hbm, index, sem)
        copy.start()
        rows[pl.ds(FACES * face_rows, mortar_ref.shape[0]), :] = mortar_ref[...]
        operand[...] = jnp.zeros_like(operand)
        copy.wait()

        def override(j, carry):
            index[fringe_ref[1, j]] = FACES * face_rows + 2 * fringe_ref[0, j]
            return carry

        lax.fori_loop(0, fringe_ref.shape[1], override, 0, unroll=8)

    @pl.when(step < extended_blocks)
    def _():
        before = step < halo_blocks
        after = step >= halo_blocks + own_blocks
        picked = []
        for v in range(variables):
            values = jnp.where(before, low_ref[v], jnp.where(after, high_ref[v], sol_ref[v]))
            picked.append(
                jnp.dot(pick_ref[...], values, preferred_element_type=jnp.float32)
            )
        pad = jnp.zeros((ROW - variables * SLOT, BLOCK), jnp.float32)
        for face in range(FACES):
            block = jnp.concatenate(
                [item[face * SLOT : (face + 1) * SLOT] for item in picked] + [pad], axis=0
            )
            turned = block.T
            start = (face ^ 1) * face_rows + pl.multiple_of(step * 2 * BLOCK, 2 * BLOCK)
            rows[pl.ds(start, BLOCK, stride=2), :] = turned[:, :LANES]
            rows[pl.ds(start + 1, BLOCK, stride=2), :] = turned[:, LANES:]

    @pl.when(step >= extended_blocks)
    def _():
        first = (step - extended_blocks) * BLOCK
        for face in range(FACES):

            def gather(chunk, carry, face=face):
                place = face * own + first + chunk * UNROLL
                held = []
                for u in range(UNROLL):
                    where = pl.multiple_of(index[place + u], 2)
                    held.append(rows[pl.ds(where, 2), :])
                target = face * 2 * BLOCK + pl.multiple_of(chunk * 2 * UNROLL, 2 * UNROLL)
                for u in range(UNROLL):
                    got[pl.ds(target + 2 * u, 2), :] = held[u]
                return carry

            lax.fori_loop(0, BLOCK // UNROLL, gather, 0)

        coupled = []
        coefficient = []
        for face in range(FACES):
            start = face * 2 * BLOCK
            block = jnp.concatenate(
                [
                    got[pl.ds(start, BLOCK, stride=2), :],
                    got[pl.ds(start + 1, BLOCK, stride=2), :],
                ],
                axis=1,
            ).astype(jnp.bfloat16)
            coupled.append(
                lax.dot_general(eye_ref[...], block, NT, preferred_element_type=jnp.float32)
            )
            speed = jnp.dot(
                pick_ref[face * SLOT : (face + 1) * SLOT],
                wind_ref[face // 2],
                preferred_element_type=jnp.float32,
            )
            speed = (2.0 * (face % 2) - 1.0) * speed
            coefficient.append(0.5 * (speed - jnp.abs(speed) - SOUND_SPEED))
        for v in range(variables):
            inside = jnp.dot(pick_ref[...], sol_ref[v], preferred_element_type=jnp.float32)
            for face in range(FACES):
                surface = (
                    inside[face * SLOT : (face + 1) * SLOT]
                    - coupled[face][v * SLOT : (v + 1) * SLOT]
                ) * coefficient[face]
                operand[v, face * SLOT : (face + 1) * SLOT, :] = surface.astype(jnp.bfloat16)
            for a in range(3):
                start = traces + a * (weight_ref.shape[1] - traces) // 3
                operand[v, start : start + nodes, :] = (
                    wind_ref[a].astype(jnp.float32) * sol_ref[v].astype(jnp.float32)
                ).astype(jnp.bfloat16)
            total = jnp.dot(weight_ref[...], operand[v], preferred_element_type=jnp.float32)
            out_ref[v] = (metric_ref[...] * total).astype(jnp.bfloat16)


def section_rate(
    solution, low, high, wind_field, metric_scale, index, fringe, mortar, weight
):
    variables, nodes, own = solution.shape
    own_blocks = own // BLOCK
    halo_blocks = BAND // BLOCK
    extended_blocks = own_blocks + 2 * halo_blocks
    face_rows = 2 * BLOCK * extended_blocks
    depth = weight.shape[1]

    def late(step):
        return jnp.maximum(step - extended_blocks, 0)

    def sol_block(step):
        early = jnp.clip(step - halo_blocks, 0, own_blocks - 1)
        return jnp.where(step < extended_blocks, early, step - extended_blocks)

    whole = pl.BlockSpec(memory_space=pltpu.VMEM)
    return pl.pallas_call(
        functools.partial(rate_kernel, halo_blocks, own_blocks),
        grid=(extended_blocks + own_blocks,),
        in_specs=[
            pl.BlockSpec(memory_space=pl.ANY),
            pl.BlockSpec(memory_space=pltpu.SMEM),
            pl.BlockSpec(
                (variables, nodes, BLOCK), lambda s: (0, 0, jnp.minimum(s, halo_blocks - 1))
            ),
            pl.BlockSpec(
                (variables, nodes, BLOCK),
                lambda s: (0, 0, jnp.clip(s - halo_blocks - own_blocks, 0, halo_blocks - 1)),
            ),
            pl.BlockSpec((variables, nodes, BLOCK), lambda s: (0, 0, sol_block(s))),
            pl.BlockSpec((3, nodes, BLOCK), lambda s: (0, 0, late(s))),
            pl.BlockSpec((1, BLOCK), lambda s: (0, late(s))),
            whole,
            whole,
            whole,
            whole,
        ],
        out_specs=pl.BlockSpec((variables, nodes, BLOCK), lambda s: (0, 0, late(s))),
        out_shape=jax.ShapeDtypeStruct(solution.shape, jnp.bfloat16),
        scratch_shapes=[
            pltpu.VMEM((FACES * face_rows + mortar.shape[0], LANES), jnp.float32),
            pltpu.VMEM((FACES * 2 * BLOCK, LANES), jnp.float32),
            pltpu.VMEM((variables, depth, BLOCK), jnp.bfloat16),
            pltpu.SMEM((FACES * own,), jnp.int32),
            pltpu.SemaphoreType.DMA,
        ],
        compiler_params=pltpu.CompilerParams(vmem_limit_bytes=58 << 20),
    )(
        index,
        fringe,
        low,
        high,
        solution,
        wind_field,
        metric_scale[None],
        mortar,
        face_picker(),
        weight,
        jnp.eye(ROW, dtype=jnp.bfloat16),
    )


def local(
    solution,
    wind_field,
    metric_scale,
    neighbours,
    precursor,
    mortar_send,
    fringe_table,
    volume_operator_stack,
    surface_lift_weight,
    mortar_proj,
):
    _, nodes, own = solution.shape
    count = lax.axis_size("elem")
    sent = mortar_rows(precursor, mortar_send, mortar_proj)
    low = lax.ppermute(solution[:, :, own - BAND :], "elem", [(i, i + 1) for i in range(count - 1)])
    high = lax.ppermute(solution[:, :, :BAND], "elem", [(i + 1, i) for i in range(count - 1)])
    arrived = lax.all_to_all(sent, "elem", split_axis=0, concat_axis=0, tiled=True)
    mortar = arrived.astype(jnp.float32).reshape(-1, LANES)
    offsets = (own + 2 * BAND) * jnp.arange(FACES, dtype=jnp.int32)
    index = (2 * (neighbours + offsets[:, None])).reshape(-1)
    lift = jnp.pad(
        surface_lift_weight.reshape(nodes, FACES, FACE_NODES),
        ((0, 0), (0, 0), (0, SLOT - FACE_NODES)),
    ).reshape(nodes, FACES * SLOT)
    volume = jnp.pad(-volume_operator_stack, ((0, 0), (0, 0), (0, 8)))
    weight = jnp.concatenate([lift] + [volume[a] for a in range(3)], axis=1)
    return section_rate(
        solution, low, high, wind_field, metric_scale, index, fringe_table[:2], mortar, weight
    )


def solution(mesh):
    in_specs = (
        P(None, None, "elem"),
        P(None, None, "elem"),
        P("elem"),
        P(None, "elem"),
        P(None, None, "elem"),
        P("elem", None, None),
        P(None, "elem"),
        P(),
        P(),
        P(),
    )
    out_specs = P(None, None, "elem")
    return jax.shard_map(local, mesh=mesh, in_specs=in_specs, out_specs=out_specs, check_vma=False)
```

```python
import functools

import jax
import jax.numpy as jnp
import numpy as np
from jax import lax
from jax.experimental import pallas as pl
from jax.experimental.pallas import tpu as pltpu
from jax.sharding import PartitionSpec as P

EDGE = 6
FACES = 6
FACE_NODES = 36
SLOT = 48
TRACES = FACES * SLOT
DEPTH = 224
LANES = 128
ROW = 2 * LANES
BAND = 512
BLOCK = 256
GROUP = 32
FETCH = 1024
KINDS = 4
SOUND_SPEED = 1.0


def face_node_lists():
    grid = np.arange(EDGE**3).reshape(EDGE, EDGE, EDGE)
    end = EDGE - 1
    return [
        grid[0].ravel(),
        grid[end].ravel(),
        grid[:, 0].ravel(),
        grid[:, end].ravel(),
        grid[:, :, 0].ravel(),
        grid[:, :, end].ravel(),
    ]


def outer_nodes():
    return np.unique(np.concatenate(face_node_lists()))


def one_hot_rows(rows, columns, places):
    pick = np.zeros((rows, columns), np.float32)
    for row, column in places:
        pick[row, column] = 1.0
    return jnp.asarray(pick, dtype=jnp.bfloat16)


def face_picker(nodes):
    position = {int(node): place for place, node in enumerate(nodes)}
    places = [
        (face * SLOT + q, position[int(node)])
        for face, held in enumerate(face_node_lists())
        for q, node in enumerate(held)
    ]
    return one_hot_rows(TRACES, len(nodes), places)


def band_kernel(pick_ref, last_ref, first_ref, last_out, first_out):
    for v in range(last_ref.shape[0]):
        for source, target in ((last_ref, last_out), (first_ref, first_out)):
            target[v] = jnp.dot(
                pick_ref[...], source[v], preferred_element_type=jnp.float32
            ).astype(jnp.bfloat16)


def band_nodes(solution):
    variables, nodes, own = solution.shape
    outer = outer_nodes()
    pick = one_hot_rows(len(outer), nodes, list(enumerate(outer)))
    band = jax.ShapeDtypeStruct((variables, len(outer), BAND), jnp.bfloat16)
    return pl.pallas_call(
        band_kernel,
        grid=(1,),
        in_specs=[
            pl.BlockSpec(pick.shape, lambda s: (0, 0)),
            pl.BlockSpec((variables, nodes, BAND), lambda s: (0, 0, own // BAND - 1)),
            pl.BlockSpec((variables, nodes, BAND), lambda s: (0, 0, 0)),
        ],
        out_specs=[pl.BlockSpec(band.shape, lambda s: (0, 0, 0))] * 2,
        out_shape=[band] * 2,
        compiler_params=pltpu.CompilerParams(vmem_limit_bytes=60 << 20),
    )(pick, solution, solution)


def mortar_kernel(
    _, __, send_ref, precursor_ref, proj_ref, lift_ref, volume_ref, out_ref, weight_ref
):
    variables, nodes, count = precursor_ref.shape
    slots = send_ref.shape[2]
    combo = jnp.maximum(send_ref[0, 0:1], 0) + send_ref[0, 1:2] * count
    ids = lax.broadcasted_iota(jnp.int32, (count, slots), 0)
    gap = jnp.zeros((SLOT - FACE_NODES, count), jnp.float32)
    pad = jnp.zeros((ROW - variables * SLOT, count), jnp.bfloat16)
    total = jnp.zeros((ROW, slots), jnp.float32)
    for kind in range(KINDS):
        pieces = []
        for v in range(variables):
            projected = jnp.dot(
                proj_ref[kind], precursor_ref[v], preferred_element_type=jnp.float32
            )
            pieces.append(jnp.concatenate([projected, gap], axis=0).astype(jnp.bfloat16))
        table = jnp.concatenate(pieces + [pad], axis=0)
        onehot = (combo == ids + kind * count).astype(jnp.float32).astype(jnp.bfloat16)
        total = total + jnp.dot(table, onehot, preferred_element_type=jnp.float32)
    out_ref[...] = total.T.astype(jnp.bfloat16)

    width = weight_ref.shape[1]
    row = lax.broadcasted_iota(jnp.int32, (nodes, width), 0)
    column = lax.broadcasted_iota(jnp.int32, (nodes, width), 1)

    def spread(matrix, places):
        place = (column == places).astype(jnp.float32).astype(jnp.bfloat16)
        return jnp.dot(matrix, place, preferred_element_type=jnp.float32)

    weight = spread(lift_ref[...], row + (SLOT - FACE_NODES) * (row // FACE_NODES))
    for a in range(3):
        weight = weight - spread(volume_ref[a], row + TRACES + a * DEPTH)
    weight_ref[...] = weight.astype(jnp.bfloat16)


def mortar_rows(band, index, precursor, mortar_send, mortar_proj, lift, volume):
    nodes = precursor.shape[1]
    whole = pl.BlockSpec(memory_space=pltpu.VMEM)
    return pl.pallas_call(
        mortar_kernel,
        in_specs=[pl.BlockSpec(memory_space=pl.ANY)] * 2 + [whole] * 5,
        out_shape=[
            jax.ShapeDtypeStruct((mortar_send.shape[2], ROW), jnp.bfloat16),
            jax.ShapeDtypeStruct((nodes, TRACES + 3 * DEPTH), jnp.bfloat16),
        ],
        compiler_params=pltpu.CompilerParams(vmem_limit_bytes=60 << 20),
    )(band, index, mortar_send, precursor, mortar_proj, lift, volume)


def rate_kernel(
    index_hbm,
    fringe_ref,
    low_hbm,
    high_hbm,
    sol_hbm,
    wind_ref,
    metric_ref,
    mortar_ref,
    pick_ref,
    pick_outer_ref,
    weight_ref,
    out_ref,
    rows,
    got_even,
    got_odd,
    operand,
    sol,
    halo,
    index,
    sems,
):
    step = pl.program_id(0)
    variables, nodes, own = sol.shape
    face_rows = 2 * (own + 2 * BAND)

    def build(values, pick, block):
        picked = [
            jnp.dot(pick, item, preferred_element_type=jnp.float32).astype(jnp.bfloat16)
            for item in values
        ]
        pad = jnp.zeros((ROW - variables * SLOT, BLOCK), jnp.bfloat16)
        for face in range(FACES):
            turned = jnp.concatenate(
                [item[face * SLOT : (face + 1) * SLOT] for item in picked] + [pad], axis=0
            ).T.astype(jnp.float32)
            start = (face ^ 1) * face_rows + pl.multiple_of(block * 2 * BLOCK, 2 * BLOCK)
            rows[pl.ds(start, BLOCK, stride=2), :] = turned[:, :LANES]
            rows[pl.ds(start + 1, BLOCK, stride=2), :] = turned[:, LANES:]

    def gather_groups(first, got):
        def group(face, chunk):
            places = index.at[pl.ds(face * own + first + chunk * GROUP, GROUP)]
            held = [rows[pl.ds(pl.multiple_of(places[u], 2), 2), :] for u in range(GROUP)]
            target = 2 * (face * BLOCK + chunk * GROUP)
            for u in range(GROUP):
                got[target + 2 * u : target + 2 * u + 2, :] = held[u]

        for face in range(FACES):
            for chunk in range(BLOCK // GROUP):
                yield group(face, chunk)

    def emit(groups, count):
        for _ in range(count):
            next(groups, None)

    def compute(part, got, groups):
        inner = slice(part * BLOCK, (part + 1) * BLOCK)
        block = pl.ds(pl.multiple_of((2 * step + part) * BLOCK, BLOCK), BLOCK)
        coupled = []
        coefficient = []
        for face in range(FACES):
            start = face * 2 * BLOCK
            fetched = jnp.concatenate(
                [
                    got[pl.ds(start, BLOCK, stride=2), :],
                    got[pl.ds(start + 1, BLOCK, stride=2), :],
                ],
                axis=1,
            ).astype(jnp.bfloat16)
            coupled.append(fetched.T)
            speed = jnp.dot(
                pick_ref[face * SLOT : (face + 1) * SLOT],
                wind_ref[face // 2, :, inner],
                preferred_element_type=jnp.float32,
            )
            emit(groups, 1)
            speed = (2.0 * (face % 2) - 1.0) * speed
            coefficient.append(0.5 * (speed - jnp.abs(speed) - SOUND_SPEED))
            emit(groups, 1)
        for v in range(variables):
            values = sol[v, :, block]
            inside = jnp.dot(pick_ref[...], values, preferred_element_type=jnp.float32)
            emit(groups, 1)
            for face in range(FACES):
                surface = (
                    inside[face * SLOT : (face + 1) * SLOT]
                    - coupled[face][v * SLOT : (v + 1) * SLOT].astype(jnp.float32)
                ) * coefficient[face]
                operand[v, face * SLOT : (face + 1) * SLOT, :] = surface.astype(jnp.bfloat16)
                if face % 2:
                    emit(groups, 1)
            for a in range(3):
                start = TRACES + a * DEPTH
                operand[v, start : start + nodes, :] = wind_ref[a, :, inner] * values
                emit(groups, 1)
            total = jnp.dot(weight_ref[...], operand[v], preferred_element_type=jnp.float32)
            out_ref[v, :, inner] = (metric_ref[:, inner] * total).astype(jnp.bfloat16)
        for _ in groups:
            pass

    @pl.when(step == 0)
    def _():
        fetches = [
            pltpu.make_async_copy(
                sol_hbm.at[:, :, c * FETCH : (c + 1) * FETCH],
                sol.at[:, :, c * FETCH : (c + 1) * FETCH],
                sems.at[c],
            )
            for c in range(own // FETCH)
        ]
        last = own // FETCH
        index_copy = pltpu.make_async_copy(index_hbm, index, sems.at[last])
        low_copy = pltpu.make_async_copy(low_hbm, halo.at[0], sems.at[last + 1])
        high_copy = pltpu.make_async_copy(high_hbm, halo.at[1], sems.at[last + 2])
        index_copy.start()
        for copy in fetches:
            copy.start()
        low_copy.start()
        high_copy.start()

        operand[...] = jnp.zeros_like(operand)
        slots = mortar_ref.shape[0]
        mortar = mortar_ref[...].astype(jnp.float32)
        rows[pl.ds(FACES * face_rows, slots, stride=2), :] = mortar[:, :LANES]
        rows[pl.ds(FACES * face_rows + 1, slots, stride=2), :] = mortar[:, LANES:]
        index_copy.wait()

        def override(j, carry):
            index[fringe_ref[1, j]] = FACES * face_rows + 2 * fringe_ref[0, j]
            return carry

        lax.fori_loop(0, fringe_ref.shape[1], override, 0, unroll=8)

        for c, copy in enumerate(fetches):
            copy.wait()

            def build_own(i, carry, c=c):
                block = c * (FETCH // BLOCK) + i
                lanes = pl.ds(pl.multiple_of(block * BLOCK, BLOCK), BLOCK)
                build(
                    [sol[v, :, lanes] for v in range(variables)],
                    pick_ref[...],
                    block + BAND // BLOCK,
                )
                return carry

            lax.fori_loop(0, FETCH // BLOCK, build_own, 0, unroll=2)
        low_copy.wait()
        high_copy.wait()
        for side, first in ((0, 0), (1, (BAND + own) // BLOCK)):

            def build_halo(i, carry, side=side, first=first):
                lanes = pl.ds(pl.multiple_of(i * BLOCK, BLOCK), BLOCK)
                build(
                    [halo[side, v, :, lanes] for v in range(variables)],
                    pick_outer_ref[...],
                    first + i,
                )
                return carry

            lax.fori_loop(0, BAND // BLOCK, build_halo, 0, unroll=2)
        for _ in gather_groups(0, got_even):
            pass

    first = 2 * step * BLOCK
    compute(0, got_even, gather_groups(first + BLOCK, got_odd))
    following = jnp.minimum(first + 2 * BLOCK, own - BLOCK)
    compute(1, got_odd, gather_groups(following, got_even))


FACE_EMIT = 2
VAR_EMIT = 7


def section_rate(
    solution, low, high, wind_field, metric_scale, index, fringe, mortar, weight
):
    variables, nodes, own = solution.shape
    face_rows = 2 * (own + 2 * BAND)
    depth = weight.shape[1]
    outer = outer_nodes()
    width = 2 * BLOCK
    whole = pl.BlockSpec(memory_space=pltpu.VMEM)
    anywhere = pl.BlockSpec(memory_space=pl.ANY)
    return pl.pallas_call(
        rate_kernel,
        grid=(own // width,),
        in_specs=[
            anywhere,
            pl.BlockSpec(memory_space=pltpu.SMEM),
            anywhere,
            anywhere,
            anywhere,
            pl.BlockSpec((3, nodes, width), lambda s: (0, 0, s)),
            pl.BlockSpec((1, width), lambda s: (0, s)),
            whole,
            whole,
            whole,
            whole,
        ],
        out_specs=pl.BlockSpec((variables, nodes, width), lambda s: (0, 0, s)),
        out_shape=jax.ShapeDtypeStruct(solution.shape, jnp.bfloat16),
        scratch_shapes=[
            pltpu.VMEM((FACES * face_rows + 2 * mortar.shape[0], LANES), jnp.float32),
            pltpu.VMEM((FACES * 2 * BLOCK, LANES), jnp.float32),
            pltpu.VMEM((FACES * 2 * BLOCK, LANES), jnp.float32),
            pltpu.VMEM((variables, depth, BLOCK), jnp.bfloat16),
            pltpu.VMEM(solution.shape, jnp.bfloat16),
            pltpu.VMEM((2,) + low.shape, jnp.bfloat16),
            pltpu.SMEM((FACES * own,), jnp.int32),
            pltpu.SemaphoreType.DMA((own // FETCH + 3,)),
        ],
        compiler_params=pltpu.CompilerParams(vmem_limit_bytes=62 << 20),
    )(
        index,
        fringe,
        low,
        high,
        solution,
        wind_field,
        metric_scale[None],
        mortar,
        face_picker(np.arange(nodes)),
        face_picker(outer),
        weight,
    )


def local(
    solution,
    wind_field,
    metric_scale,
    neighbours,
    precursor,
    mortar_send,
    fringe_table,
    volume_operator_stack,
    surface_lift_weight,
    mortar_proj,
):
    own = solution.shape[2]
    count = lax.axis_size("elem")
    last, first = band_nodes(solution)
    low = lax.ppermute(last, "elem", [(i, i + 1) for i in range(count - 1)])
    high = lax.ppermute(first, "elem", [(i + 1, i) for i in range(count - 1)])
    offsets = (own + 2 * BAND) * jnp.arange(FACES, dtype=jnp.int32)
    index = (2 * (neighbours + offsets[:, None])).reshape(-1)
    sent, weight = mortar_rows(
        last,
        index,
        precursor,
        mortar_send,
        mortar_proj,
        surface_lift_weight,
        volume_operator_stack,
    )
    mortar = lax.all_to_all(sent, "elem", split_axis=0, concat_axis=0, tiled=True)
    return section_rate(
        solution, low, high, wind_field, metric_scale, index, fringe_table, mortar, weight
    )


def solution(mesh):
    in_specs = (
        P(None, None, "elem"),
        P(None, None, "elem"),
        P("elem"),
        P(None, "elem"),
        P(None, None, "elem"),
        P("elem", None, None),
        P(None, "elem"),
        P(),
        P(),
        P(),
    )
    out_specs = P(None, None, "elem")
    return jax.shard_map(local, mesh=mesh, in_specs=in_specs, out_specs=out_specs, check_vma=False)
```

```python
import functools

import jax
import jax.numpy as jnp
import numpy as np
from jax import lax
from jax.experimental import pallas as pl
from jax.experimental.pallas import tpu as pltpu
from jax.sharding import PartitionSpec as P

EDGE = 6
FACES = 6
FACE_NODES = 36
SLOT = 48
TIGHT = 40
LANES = 128
ROW = 2 * LANES
BAND = 512
BLOCK = 256
GROUP = 32
FETCH = 1024
KINDS = 4
SOUND_SPEED = 1.0


def face_node_lists():
    grid = np.arange(EDGE**3).reshape(EDGE, EDGE, EDGE)
    end = EDGE - 1
    return [
        grid[0].ravel(),
        grid[end].ravel(),
        grid[:, 0].ravel(),
        grid[:, end].ravel(),
        grid[:, :, 0].ravel(),
        grid[:, :, end].ravel(),
    ]


def outer_nodes():
    return np.unique(np.concatenate(face_node_lists()))


def one_hot_rows(rows, columns, places):
    pick = np.zeros((rows, columns), np.float32)
    for row, column in places:
        pick[row, column] = 1.0
    return jnp.asarray(pick, dtype=jnp.bfloat16)


def face_picker(nodes, slot):
    position = {int(node): place for place, node in enumerate(nodes)}
    places = [
        (face * slot + q, position[int(node)])
        for face, held in enumerate(face_node_lists())
        for q, node in enumerate(held)
    ]
    return one_hot_rows(FACES * slot, len(nodes), places)


def band_kernel(_, pick_ref, last_ref, first_ref, last_out, first_out):
    for v in range(last_ref.shape[0]):
        for source, target in ((last_ref, last_out), (first_ref, first_out)):
            target[v] = jnp.dot(
                pick_ref[...], source[v], preferred_element_type=jnp.float32
            ).astype(jnp.bfloat16)


def band_nodes(after, solution):
    variables, nodes, own = solution.shape
    outer = outer_nodes()
    pick = one_hot_rows(len(outer), nodes, list(enumerate(outer)))
    band = jax.ShapeDtypeStruct((variables, len(outer), BAND), jnp.bfloat16)
    return pl.pallas_call(
        band_kernel,
        grid=(1,),
        in_specs=[
            pl.BlockSpec(memory_space=pl.ANY),
            pl.BlockSpec(pick.shape, lambda s: (0, 0)),
            pl.BlockSpec((variables, nodes, BAND), lambda s: (0, 0, own // BAND - 1)),
            pl.BlockSpec((variables, nodes, BAND), lambda s: (0, 0, 0)),
        ],
        out_specs=[pl.BlockSpec(band.shape, lambda s: (0, 0, 0))] * 2,
        out_shape=[band] * 2,
        compiler_params=pltpu.CompilerParams(vmem_limit_bytes=60 << 20),
    )(after, pick, solution, solution)


def mortar_kernel(
    send_ref, precursor_ref, proj_ref, lift_ref, out_ref, weight_ref
):
    variables, nodes, count = precursor_ref.shape
    slots = send_ref.shape[2]
    combo = jnp.maximum(send_ref[0, 0:1], 0) + send_ref[0, 1:2] * count
    ids = lax.broadcasted_iota(jnp.int32, (count, slots), 0)
    gap = jnp.zeros((SLOT - FACE_NODES, count), jnp.float32)
    pad = jnp.zeros((ROW - variables * SLOT, count), jnp.bfloat16)
    total = jnp.zeros((ROW, slots), jnp.float32)
    for kind in range(KINDS):
        pieces = []
        for v in range(variables):
            projected = jnp.dot(
                proj_ref[kind], precursor_ref[v], preferred_element_type=jnp.float32
            )
            pieces.append(jnp.concatenate([projected, gap], axis=0).astype(jnp.bfloat16))
        table = jnp.concatenate(pieces + [pad], axis=0)
        onehot = (combo == ids + kind * count).astype(jnp.float32).astype(jnp.bfloat16)
        total = total + jnp.dot(table, onehot, preferred_element_type=jnp.float32)
    out_ref[...] = total.T.astype(jnp.bfloat16)

    width = weight_ref.shape[1]
    row = lax.broadcasted_iota(jnp.int32, (nodes, width), 0)
    column = lax.broadcasted_iota(jnp.int32, (nodes, width), 1)

    places = row + (TIGHT - FACE_NODES) * (row // FACE_NODES)
    place = (column == places).astype(jnp.float32).astype(jnp.bfloat16)
    weight_ref[...] = jnp.dot(
        lift_ref[...], place, preferred_element_type=jnp.float32
    ).astype(jnp.bfloat16)


def mortar_rows(precursor, mortar_send, mortar_proj, lift):
    nodes = precursor.shape[1]
    whole = pl.BlockSpec(memory_space=pltpu.VMEM)
    return pl.pallas_call(
        mortar_kernel,
        in_specs=[whole] * 4,
        out_shape=[
            jax.ShapeDtypeStruct((mortar_send.shape[2], ROW), jnp.bfloat16),
            jax.ShapeDtypeStruct((nodes, FACES * TIGHT), jnp.bfloat16),
        ],
        compiler_params=pltpu.CompilerParams(vmem_limit_bytes=60 << 20),
    )(mortar_send, precursor, mortar_proj, lift)


def volume_kernel(_, sol_ref, wind_ref, pick_ref, operator_ref, volume_ref, speed_ref):
    for face in range(FACES):
        speed = jnp.dot(
            pick_ref[face * SLOT : (face + 1) * SLOT],
            wind_ref[face // 2],
            preferred_element_type=jnp.float32,
        )
        speed_ref[face * SLOT : (face + 1) * SLOT] = (
            (2.0 * (face % 2) - 1.0) * speed
        ).astype(jnp.bfloat16)
    for v in range(sol_ref.shape[0]):
        parts = [
            jnp.dot(operator_ref[a], wind_ref[a] * sol_ref[v], preferred_element_type=jnp.float32)
            for a in range(3)
        ]
        volume_ref[v] = parts[0] + parts[1] + parts[2]


def volume_terms(band, solution, wind_field, operators):
    variables, nodes, own = solution.shape
    width = 2 * BLOCK
    whole = pl.BlockSpec(memory_space=pltpu.VMEM)
    return pl.pallas_call(
        volume_kernel,
        grid=(own // width,),
        in_specs=[
            pl.BlockSpec(memory_space=pl.ANY),
            pl.BlockSpec((variables, nodes, width), lambda s: (0, 0, s)),
            pl.BlockSpec((3, nodes, width), lambda s: (0, 0, s)),
            whole,
            whole,
        ],
        out_specs=[
            pl.BlockSpec((variables, nodes, width), lambda s: (0, 0, s)),
            pl.BlockSpec((FACES * SLOT, width), lambda s: (0, s)),
        ],
        out_shape=[
            jax.ShapeDtypeStruct(solution.shape, jnp.float32),
            jax.ShapeDtypeStruct((FACES * SLOT, own), jnp.bfloat16),
        ],
        cost_estimate=pl.CostEstimate(
            flops=6 * variables * nodes * nodes * own,
            bytes_accessed=40 * nodes * own,
            transcendentals=0,
        ),
        compiler_params=pltpu.CompilerParams(vmem_limit_bytes=60 << 20),
    )(band, solution, wind_field, face_picker(np.arange(nodes), SLOT), operators)


def rate_kernel(
    index_hbm,
    fringe_ref,
    low_hbm,
    high_hbm,
    sol_hbm,
    volume_ref,
    speed_ref,
    metric_ref,
    mortar_ref,
    pick_ref,
    pick_outer_ref,
    pick_tight_ref,
    weight_ref,
    out_ref,
    rows,
    got_even,
    got_odd,
    sol,
    halo,
    index,
    sems,
):
    step = pl.program_id(0)
    variables, nodes, own = sol.shape
    face_rows = 2 * (own + 2 * BAND)

    def build(values, pick, block):
        picked = [
            jnp.dot(pick, item, preferred_element_type=jnp.float32).astype(jnp.bfloat16)
            for item in values
        ]
        pad = jnp.zeros((ROW - variables * SLOT, BLOCK), jnp.bfloat16)
        for face in range(FACES):
            turned = jnp.concatenate(
                [item[face * SLOT : (face + 1) * SLOT] for item in picked] + [pad], axis=0
            ).T.astype(jnp.float32)
            start = (face ^ 1) * face_rows + pl.multiple_of(block * 2 * BLOCK, 2 * BLOCK)
            rows[pl.ds(start, BLOCK, stride=2), :] = turned[:, :LANES]
            rows[pl.ds(start + 1, BLOCK, stride=2), :] = turned[:, LANES:]

    def gather_groups(first, got):
        def group(face, chunk):
            places = index.at[pl.ds(face * own + first + chunk * GROUP, GROUP)]
            held = [rows[pl.ds(pl.multiple_of(places[u], 2), 2), :] for u in range(GROUP)]
            target = 2 * (face * BLOCK + chunk * GROUP)
            for u in range(GROUP):
                got[target + 2 * u : target + 2 * u + 2, :] = held[u]

        for face in range(FACES):
            for chunk in range(BLOCK // GROUP):
                yield group(face, chunk)

    def emit(groups, count):
        for _ in range(count):
            next(groups, None)

    def compute(part, got, groups):
        inner = slice(part * BLOCK, (part + 1) * BLOCK)
        block = pl.ds(pl.multiple_of((2 * step + part) * BLOCK, BLOCK), BLOCK)
        coupled = []
        coefficient = []
        for face in range(FACES):
            start = face * 2 * BLOCK
            fetched = jnp.concatenate(
                [
                    got[pl.ds(start, BLOCK, stride=2), :],
                    got[pl.ds(start + 1, BLOCK, stride=2), :],
                ],
                axis=1,
            ).astype(jnp.bfloat16)
            coupled.append(fetched.T)
            speed = speed_ref[face * SLOT : (face + 1) * SLOT, inner].astype(jnp.float32)[:TIGHT]
            coefficient.append(0.5 * (speed - jnp.abs(speed) - SOUND_SPEED))
            emit(groups, 3)
        for v in range(variables):
            inside = jnp.dot(
                pick_tight_ref[...], sol[v, :, block], preferred_element_type=jnp.float32
            )
            pieces = []
            for face in range(FACES):
                beyond = coupled[face][v * SLOT : (v + 1) * SLOT].astype(jnp.float32)[:TIGHT]
                tight = slice(face * TIGHT, (face + 1) * TIGHT)
                pieces.append((inside[tight] - beyond) * coefficient[face])
                emit(groups, 1)
            surface = jnp.concatenate(pieces, axis=0).astype(jnp.bfloat16)
            total = jnp.dot(weight_ref[...], surface, preferred_element_type=jnp.float32)
            out_ref[v, :, inner] = (
                metric_ref[:, inner] * (total - volume_ref[v, :, inner])
            ).astype(jnp.bfloat16)
        for _ in groups:
            pass

    @pl.when(step == 0)
    def _():
        fetches = [
            pltpu.make_async_copy(
                sol_hbm.at[:, :, c * FETCH : (c + 1) * FETCH],
                sol.at[:, :, c * FETCH : (c + 1) * FETCH],
                sems.at[c],
            )
            for c in range(own // FETCH)
        ]
        last = own // FETCH
        index_copy = pltpu.make_async_copy(index_hbm, index, sems.at[last])
        low_copy = pltpu.make_async_copy(low_hbm, halo.at[0], sems.at[last + 1])
        high_copy = pltpu.make_async_copy(high_hbm, halo.at[1], sems.at[last + 2])
        index_copy.start()
        for copy in fetches:
            copy.start()
        low_copy.start()
        high_copy.start()

        slots = mortar_ref.shape[0]
        mortar = mortar_ref[...].astype(jnp.float32)
        rows[pl.ds(FACES * face_rows, slots, stride=2), :] = mortar[:, :LANES]
        rows[pl.ds(FACES * face_rows + 1, slots, stride=2), :] = mortar[:, LANES:]
        index_copy.wait()

        def override(j, carry):
            index[fringe_ref[1, j]] = FACES * face_rows + 2 * fringe_ref[0, j]
            return carry

        lax.fori_loop(0, fringe_ref.shape[1], override, 0, unroll=8)

        for c, copy in enumerate(fetches):
            copy.wait()

            def build_own(i, carry, c=c):
                block = c * (FETCH // BLOCK) + i
                lanes = pl.ds(pl.multiple_of(block * BLOCK, BLOCK), BLOCK)
                build(
                    [sol[v, :, lanes] for v in range(variables)],
                    pick_ref[...],
                    block + BAND // BLOCK,
                )
                return carry

            lax.fori_loop(0, FETCH // BLOCK, build_own, 0, unroll=2)
        low_copy.wait()
        high_copy.wait()
        for side, first in ((0, 0), (1, (BAND + own) // BLOCK)):

            def build_halo(i, carry, side=side, first=first):
                lanes = pl.ds(pl.multiple_of(i * BLOCK, BLOCK), BLOCK)
                build(
                    [halo[side, v, :, lanes] for v in range(variables)],
                    pick_outer_ref[...],
                    first + i,
                )
                return carry

            lax.fori_loop(0, BAND // BLOCK, build_halo, 0, unroll=2)
        for _ in gather_groups(0, got_even):
            pass

    first = 2 * step * BLOCK
    compute(0, got_even, gather_groups(first + BLOCK, got_odd))

    @pl.when(step >= 0)
    def _():
        following = jnp.minimum(first + 2 * BLOCK, own - BLOCK)
        compute(1, got_odd, gather_groups(following, got_even))


def section_rate(
    solution, low, high, volume, speed, metric_scale, index, fringe, mortar, weight
):
    variables, nodes, own = solution.shape
    face_rows = 2 * (own + 2 * BAND)
    outer = outer_nodes()
    width = 2 * BLOCK
    whole = pl.BlockSpec(memory_space=pltpu.VMEM)
    anywhere = pl.BlockSpec(memory_space=pl.ANY)
    return pl.pallas_call(
        rate_kernel,
        grid=(own // width,),
        in_specs=[
            anywhere,
            pl.BlockSpec(memory_space=pltpu.SMEM),
            anywhere,
            anywhere,
            anywhere,
            pl.BlockSpec((variables, nodes, width), lambda s: (0, 0, s)),
            pl.BlockSpec((FACES * SLOT, width), lambda s: (0, s)),
            pl.BlockSpec((1, width), lambda s: (0, s)),
            whole,
            whole,
            whole,
            whole,
            whole,
        ],
        out_specs=pl.BlockSpec((variables, nodes, width), lambda s: (0, 0, s)),
        out_shape=jax.ShapeDtypeStruct(solution.shape, jnp.bfloat16),
        scratch_shapes=[
            pltpu.VMEM((FACES * face_rows + 2 * mortar.shape[0], LANES), jnp.float32),
            pltpu.VMEM((FACES * 2 * BLOCK, LANES), jnp.float32),
            pltpu.VMEM((FACES * 2 * BLOCK, LANES), jnp.float32),
            pltpu.VMEM(solution.shape, jnp.bfloat16),
            pltpu.VMEM((2,) + low.shape, jnp.bfloat16),
            pltpu.SMEM((FACES * own,), jnp.int32),
            pltpu.SemaphoreType.DMA((own // FETCH + 3,)),
        ],
        compiler_params=pltpu.CompilerParams(vmem_limit_bytes=62 << 20),
    )(
        index,
        fringe,
        low,
        high,
        solution,
        volume,
        speed,
        metric_scale[None],
        mortar,
        face_picker(np.arange(nodes), SLOT),
        face_picker(outer, SLOT),
        face_picker(np.arange(nodes), TIGHT),
        weight,
    )


def local(
    solution,
    wind_field,
    metric_scale,
    neighbours,
    precursor,
    mortar_send,
    fringe_table,
    volume_operator_stack,
    surface_lift_weight,
    mortar_proj,
):
    own = solution.shape[2]
    count = lax.axis_size("elem")
    sent, weight = mortar_rows(precursor, mortar_send, mortar_proj, surface_lift_weight)
    mortar = lax.all_to_all(sent, "elem", split_axis=0, concat_axis=0, tiled=True)
    last, first = band_nodes(sent, solution)
    low = lax.ppermute(last, "elem", [(i, i + 1) for i in range(count - 1)])
    high = lax.ppermute(first, "elem", [(i + 1, i) for i in range(count - 1)])
    volume, speed = volume_terms(last, solution, wind_field, volume_operator_stack)
    offsets = (own + 2 * BAND) * jnp.arange(FACES, dtype=jnp.int32)
    index = (2 * (neighbours + offsets[:, None])).reshape(-1)
    return section_rate(
        solution,
        low,
        high,
        volume,
        speed,
        metric_scale,
        index,
        fringe_table,
        mortar,
        weight,
    )


def solution(mesh):
    in_specs = (
        P(None, None, "elem"),
        P(None, None, "elem"),
        P("elem"),
        P(None, "elem"),
        P(None, None, "elem"),
        P("elem", None, None),
        P(None, "elem"),
        P(),
        P(),
        P(),
    )
    out_specs = P(None, None, "elem")
    return jax.shard_map(local, mesh=mesh, in_specs=in_specs, out_specs=out_specs, check_vma=False)
```

```python
import functools

import jax
import jax.numpy as jnp
import numpy as np
from jax import lax
from jax.experimental import pallas as pl
from jax.experimental.pallas import tpu as pltpu
from jax.sharding import PartitionSpec as P

EDGE = 6
FACES = 6
FACE_NODES = 36
SLOT = 48
TIGHT = 40
LANES = 128
ROW = 2 * LANES
BAND = 512
BLOCK = 256
GROUP = 8
FETCH = 1024
KINDS = 4
SOUND_SPEED = 1.0


def face_node_lists():
    grid = np.arange(EDGE**3).reshape(EDGE, EDGE, EDGE)
    end = EDGE - 1
    return [
        grid[0].ravel(),
        grid[end].ravel(),
        grid[:, 0].ravel(),
        grid[:, end].ravel(),
        grid[:, :, 0].ravel(),
        grid[:, :, end].ravel(),
    ]


def outer_nodes():
    return np.unique(np.concatenate(face_node_lists()))


def one_hot_rows(rows, columns, places):
    pick = np.zeros((rows, columns), np.float32)
    for row, column in places:
        pick[row, column] = 1.0
    return jnp.asarray(pick, dtype=jnp.bfloat16)


def face_picker(nodes, slot):
    position = {int(node): place for place, node in enumerate(nodes)}
    places = [
        (face * slot + q, position[int(node)])
        for face, held in enumerate(face_node_lists())
        for q, node in enumerate(held)
    ]
    return one_hot_rows(FACES * slot, len(nodes), places)


def band_kernel(_, pick_ref, last_ref, first_ref, last_out, first_out):
    for v in range(last_ref.shape[0]):
        for source, target in ((last_ref, last_out), (first_ref, first_out)):
            target[v] = jnp.dot(
                pick_ref[...], source[v], preferred_element_type=jnp.float32
            ).astype(jnp.bfloat16)


def band_nodes(after, solution):
    variables, nodes, own = solution.shape
    outer = outer_nodes()
    pick = one_hot_rows(len(outer), nodes, list(enumerate(outer)))
    band = jax.ShapeDtypeStruct((variables, len(outer), BAND), jnp.bfloat16)
    return pl.pallas_call(
        band_kernel,
        grid=(1,),
        in_specs=[
            pl.BlockSpec(memory_space=pl.ANY),
            pl.BlockSpec(pick.shape, lambda s: (0, 0)),
            pl.BlockSpec((variables, nodes, BAND), lambda s: (0, 0, own // BAND - 1)),
            pl.BlockSpec((variables, nodes, BAND), lambda s: (0, 0, 0)),
        ],
        out_specs=[pl.BlockSpec(band.shape, lambda s: (0, 0, 0))] * 2,
        out_shape=[band] * 2,
        compiler_params=pltpu.CompilerParams(vmem_limit_bytes=60 << 20),
    )(after, pick, solution, solution)


def mortar_kernel(
    send_ref, precursor_ref, proj_ref, lift_ref, out_ref, weight_ref
):
    variables, nodes, count = precursor_ref.shape
    slots = send_ref.shape[2]
    combo = jnp.maximum(send_ref[0, 0:1], 0) + send_ref[0, 1:2] * count
    ids = lax.broadcasted_iota(jnp.int32, (count, slots), 0)
    gap = jnp.zeros((SLOT - FACE_NODES, count), jnp.float32)
    pad = jnp.zeros((ROW - variables * SLOT, count), jnp.bfloat16)
    total = jnp.zeros((ROW, slots), jnp.float32)
    for kind in range(KINDS):
        pieces = []
        for v in range(variables):
            projected = jnp.dot(
                proj_ref[:, kind, :], precursor_ref[v], preferred_element_type=jnp.float32
            )
            pieces.append(jnp.concatenate([projected, gap], axis=0).astype(jnp.bfloat16))
        table = jnp.concatenate(pieces + [pad], axis=0)
        onehot = (combo == ids + kind * count).astype(jnp.float32).astype(jnp.bfloat16)
        total = total + jnp.dot(table, onehot, preferred_element_type=jnp.float32)
    out_ref[...] = total.T.astype(jnp.bfloat16)

    width = weight_ref.shape[1]
    row = lax.broadcasted_iota(jnp.int32, (nodes, width), 0)
    column = lax.broadcasted_iota(jnp.int32, (nodes, width), 1)

    places = row + (TIGHT - FACE_NODES) * (row // FACE_NODES)
    place = (column == places).astype(jnp.float32).astype(jnp.bfloat16)
    weight_ref[...] = jnp.dot(
        lift_ref[...], place, preferred_element_type=jnp.float32
    ).astype(jnp.bfloat16)


def mortar_rows(precursor, mortar_send, mortar_proj, lift):
    nodes = precursor.shape[1]
    whole = pl.BlockSpec(memory_space=pltpu.VMEM)
    return pl.pallas_call(
        mortar_kernel,
        in_specs=[whole] * 4,
        out_shape=[
            jax.ShapeDtypeStruct((mortar_send.shape[2], ROW), jnp.bfloat16),
            jax.ShapeDtypeStruct((nodes, FACES * TIGHT), jnp.bfloat16),
        ],
        compiler_params=pltpu.CompilerParams(vmem_limit_bytes=60 << 20),
    )(mortar_send, precursor, mortar_proj.transpose(1, 0, 2), lift)


def volume_kernel(_, sol_ref, wind_ref, pick_ref, operator_ref, volume_ref, speed_ref):
    for face in range(FACES):
        speed = jnp.dot(
            pick_ref[face * SLOT : (face + 1) * SLOT],
            wind_ref[face // 2],
            preferred_element_type=jnp.float32,
        )
        speed_ref[face * SLOT : (face + 1) * SLOT] = (
            (2.0 * (face % 2) - 1.0) * speed
        ).astype(jnp.bfloat16)
    for v in range(sol_ref.shape[0]):
        parts = [
            jnp.dot(operator_ref[a], wind_ref[a] * sol_ref[v], preferred_element_type=jnp.float32)
            for a in range(3)
        ]
        volume_ref[v] = parts[0] + parts[1] + parts[2]


def volume_terms(band, solution, wind_field, operators):
    variables, nodes, own = solution.shape
    width = 2 * BLOCK
    whole = pl.BlockSpec(memory_space=pltpu.VMEM)
    return pl.pallas_call(
        volume_kernel,
        grid=(own // width,),
        in_specs=[
            pl.BlockSpec(memory_space=pl.ANY),
            pl.BlockSpec((variables, nodes, width), lambda s: (0, 0, s)),
            pl.BlockSpec((3, nodes, width), lambda s: (0, 0, s)),
            whole,
            whole,
        ],
        out_specs=[
            pl.BlockSpec((variables, nodes, width), lambda s: (0, 0, s)),
            pl.BlockSpec((FACES * SLOT, width), lambda s: (0, s)),
        ],
        out_shape=[
            jax.ShapeDtypeStruct(solution.shape, jnp.float32),
            jax.ShapeDtypeStruct((FACES * SLOT, own), jnp.bfloat16),
        ],
        cost_estimate=pl.CostEstimate(
            flops=6 * variables * nodes * nodes * own,
            bytes_accessed=40 * nodes * own,
            transcendentals=0,
        ),
        compiler_params=pltpu.CompilerParams(vmem_limit_bytes=60 << 20),
    )(band, solution, wind_field, face_picker(np.arange(nodes), SLOT), operators)


def rate_kernel(
    index_hbm,
    fringe_ref,
    low_hbm,
    high_hbm,
    sol_hbm,
    volume_ref,
    speed_ref,
    metric_ref,
    mortar_ref,
    pick_ref,
    pick_outer_ref,
    pick_tight_ref,
    weight_ref,
    out_ref,
    rows,
    got_even,
    got_odd,
    sol,
    halo,
    index,
    sems,
):
    step = pl.program_id(0)
    variables, nodes, own = sol.shape
    face_rows = 2 * (own + 2 * BAND)

    def build(values, pick, block):
        picked = [
            jnp.dot(pick, item, preferred_element_type=jnp.float32).astype(jnp.bfloat16)
            for item in values
        ]
        pad = jnp.zeros((ROW - variables * SLOT, BLOCK), jnp.bfloat16)
        for face in range(FACES):
            turned = jnp.concatenate(
                [item[face * SLOT : (face + 1) * SLOT] for item in picked] + [pad], axis=0
            ).T.astype(jnp.float32)
            start = (face ^ 1) * face_rows + pl.multiple_of(block * 2 * BLOCK, 2 * BLOCK)
            rows[pl.ds(start, BLOCK, stride=2), :] = turned[:, :LANES]
            rows[pl.ds(start + 1, BLOCK, stride=2), :] = turned[:, LANES:]

    def gather_groups(first, got):
        def group(face, chunk):
            places = index.at[pl.ds(face * own + first + chunk * GROUP, GROUP)]
            held = [rows[pl.ds(pl.multiple_of(places[u], 2), 2), :] for u in range(GROUP)]
            target = 2 * (face * BLOCK + chunk * GROUP)
            for u in range(GROUP):
                got[target + 2 * u : target + 2 * u + 2, :] = held[u]

        for face in range(FACES):
            for chunk in range(BLOCK // GROUP):
                yield group(face, chunk)

    def emit(groups, count):
        for _ in range(count):
            next(groups, None)

    def compute(part, got, groups):
        inner = slice(part * BLOCK, (part + 1) * BLOCK)
        block = pl.ds(pl.multiple_of((2 * step + part) * BLOCK, BLOCK), BLOCK)
        coupled = []
        coefficient = []
        for face in range(FACES):
            start = face * 2 * BLOCK
            fetched = jnp.concatenate(
                [
                    got[pl.ds(start, BLOCK, stride=2), :],
                    got[pl.ds(start + 1, BLOCK, stride=2), :],
                ],
                axis=1,
            ).astype(jnp.bfloat16)
            coupled.append(fetched.T)
            speed = speed_ref[face * SLOT : (face + 1) * SLOT, inner].astype(jnp.float32)[:TIGHT]
            coefficient.append(0.5 * (speed - jnp.abs(speed) - SOUND_SPEED))
        for v in range(variables):
            inside = jnp.dot(
                pick_tight_ref[...], sol[v, :, block], preferred_element_type=jnp.float32
            )
            pieces = []
            for face in range(FACES):
                beyond = coupled[face][v * SLOT : (v + 1) * SLOT].astype(jnp.float32)[:TIGHT]
                tight = slice(face * TIGHT, (face + 1) * TIGHT)
                pieces.append((inside[tight] - beyond) * coefficient[face])
                emit(groups, 7)
            surface = jnp.concatenate(pieces, axis=0).astype(jnp.bfloat16)
            total = jnp.dot(weight_ref[...], surface, preferred_element_type=jnp.float32)
            out_ref[v, :, inner] = (
                metric_ref[:, inner] * (total - volume_ref[v, :, inner])
            ).astype(jnp.bfloat16)
        for _ in groups:
            pass

    @pl.when(step == 0)
    def _():
        fetches = [
            pltpu.make_async_copy(
                sol_hbm.at[:, :, c * FETCH : (c + 1) * FETCH],
                sol.at[:, :, c * FETCH : (c + 1) * FETCH],
                sems.at[c],
            )
            for c in range(own // FETCH)
        ]
        last = own // FETCH
        index_copy = pltpu.make_async_copy(index_hbm, index, sems.at[last])
        low_copy = pltpu.make_async_copy(low_hbm, halo.at[0], sems.at[last + 1])
        high_copy = pltpu.make_async_copy(high_hbm, halo.at[1], sems.at[last + 2])
        index_copy.start()
        for copy in fetches:
            copy.start()
        low_copy.start()
        high_copy.start()

        slots = mortar_ref.shape[0]
        mortar = mortar_ref[...].astype(jnp.float32)
        rows[pl.ds(FACES * face_rows, slots, stride=2), :] = mortar[:, :LANES]
        rows[pl.ds(FACES * face_rows + 1, slots, stride=2), :] = mortar[:, LANES:]
        index_copy.wait()

        def override(j, carry):
            index[fringe_ref[1, j]] = FACES * face_rows + 2 * fringe_ref[0, j]
            return carry

        lax.fori_loop(0, fringe_ref.shape[1], override, 0, unroll=8)

        for c, copy in enumerate(fetches):
            copy.wait()

            def build_own(i, carry, c=c):
                block = c * (FETCH // BLOCK) + i
                lanes = pl.ds(pl.multiple_of(block * BLOCK, BLOCK), BLOCK)
                build(
                    [sol[v, :, lanes] for v in range(variables)],
                    pick_ref[...],
                    block + BAND // BLOCK,
                )
                return carry

            lax.fori_loop(0, FETCH // BLOCK, build_own, 0, unroll=4)
        low_copy.wait()
        high_copy.wait()
        for side, first in ((0, 0), (1, (BAND + own) // BLOCK)):

            def build_halo(i, carry, side=side, first=first):
                lanes = pl.ds(pl.multiple_of(i * BLOCK, BLOCK), BLOCK)
                build(
                    [halo[side, v, :, lanes] for v in range(variables)],
                    pick_outer_ref[...],
                    first + i,
                )
                return carry

            lax.fori_loop(0, BAND // BLOCK, build_halo, 0, unroll=2)
        for _ in gather_groups(0, got_even):
            pass

    first = 2 * step * BLOCK
    compute(0, got_even, gather_groups(first + BLOCK, got_odd))

    @pl.when(step >= 0)
    def _():
        following = jnp.minimum(first + 2 * BLOCK, own - BLOCK)
        compute(1, got_odd, gather_groups(following, got_even))


def section_rate(
    solution, low, high, volume, speed, metric_scale, index, fringe, mortar, weight
):
    variables, nodes, own = solution.shape
    face_rows = 2 * (own + 2 * BAND)
    outer = outer_nodes()
    width = 2 * BLOCK
    whole = pl.BlockSpec(memory_space=pltpu.VMEM)
    anywhere = pl.BlockSpec(memory_space=pl.ANY)
    return pl.pallas_call(
        rate_kernel,
        grid=(own // width,),
        in_specs=[
            anywhere,
            pl.BlockSpec(memory_space=pltpu.SMEM),
            anywhere,
            anywhere,
            anywhere,
            pl.BlockSpec((variables, nodes, width), lambda s: (0, 0, s)),
            pl.BlockSpec((FACES * SLOT, width), lambda s: (0, s)),
            pl.BlockSpec((1, width), lambda s: (0, s)),
            whole,
            whole,
            whole,
            whole,
            whole,
        ],
        out_specs=pl.BlockSpec((variables, nodes, width), lambda s: (0, 0, s)),
        out_shape=jax.ShapeDtypeStruct(solution.shape, jnp.bfloat16),
        scratch_shapes=[
            pltpu.VMEM((FACES * face_rows + 2 * mortar.shape[0], LANES), jnp.float32),
            pltpu.VMEM((FACES * 2 * BLOCK, LANES), jnp.float32),
            pltpu.VMEM((FACES * 2 * BLOCK, LANES), jnp.float32),
            pltpu.VMEM(solution.shape, jnp.bfloat16),
            pltpu.VMEM((2,) + low.shape, jnp.bfloat16),
            pltpu.SMEM((FACES * own,), jnp.int32),
            pltpu.SemaphoreType.DMA((own // FETCH + 3,)),
        ],
        compiler_params=pltpu.CompilerParams(vmem_limit_bytes=62 << 20),
    )(
        index,
        fringe,
        low,
        high,
        solution,
        volume,
        speed,
        metric_scale[None],
        mortar,
        face_picker(np.arange(nodes), SLOT),
        face_picker(outer, SLOT),
        face_picker(np.arange(nodes), TIGHT),
        weight,
    )


def local(
    solution,
    wind_field,
    metric_scale,
    neighbours,
    precursor,
    mortar_send,
    fringe_table,
    volume_operator_stack,
    surface_lift_weight,
    mortar_proj,
):
    own = solution.shape[2]
    count = lax.axis_size("elem")
    sent, weight = mortar_rows(precursor, mortar_send, mortar_proj, surface_lift_weight)
    mortar = lax.all_to_all(sent, "elem", split_axis=0, concat_axis=0, tiled=True)
    last, first = band_nodes(sent, solution)
    low = lax.ppermute(last, "elem", [(i, i + 1) for i in range(count - 1)])
    high = lax.ppermute(first, "elem", [(i + 1, i) for i in range(count - 1)])
    volume, speed = volume_terms(last, solution, wind_field, volume_operator_stack)
    offsets = (own + 2 * BAND) * jnp.arange(FACES, dtype=jnp.int32)
    index = (2 * (neighbours + offsets[:, None])).reshape(-1)
    return section_rate(
        solution,
        low,
        high,
        volume,
        speed,
        metric_scale,
        index,
        fringe_table,
        mortar,
        weight,
    )


def solution(mesh):
    in_specs = (
        P(None, None, "elem"),
        P(None, None, "elem"),
        P("elem"),
        P(None, "elem"),
        P(None, None, "elem"),
        P("elem", None, None),
        P(None, "elem"),
        P(),
        P(),
        P(),
    )
    out_specs = P(None, None, "elem")
    return jax.shard_map(local, mesh=mesh, in_specs=in_specs, out_specs=out_specs, check_vma=False)
```
